128 devices in a mesh: row: 8 (over y, x_hi), col: 16 (over z, x_lo, core).
Axes of the slice: x: 4 (x_hi: 2, x_lo: 2; x = x_hi * 2 + x_lo), y: 4, z: 4, core: 2. Of those that a mesh axis runs over, the one named last changes fastest.
Arguments:
- momentum: float32 [16384, 16384], P(('row', 'col')), may hold values from -1200 to 1200
Outputs:
- gram: float32 [16384, 16384], P('row', 'col')
- tiles: bfloat16 [16384, 16384], P('row', 'col')
The draws below stay inside these ranges and needn't reach their ends.
All inputs are finite; a program needn't handle non-finite values.
Results may differ from the reference program's by a relative error of at most 0.0043.
Values may be sent and summed in bfloat16 or wider, within the bound.
A program may use at most 128 MiB of HBM per device.

```python
import jax
import jax.numpy as jnp
from jax import lax

ORDER = 16384
WINDOW = 2048


def draw_momentum(key, part):
    key = jax.random.fold_in(key, 1)
    key_vals, key_rows, key_cols = jax.random.split(key, 3)
    position = jnp.arange(ORDER, dtype=jnp.float32).reshape(ORDER, 1)
    rising = jnp.exp(jnp.log(3.0) * position / ORDER)
    row_scale = rising * 10.0 ** jax.random.uniform(key_rows, (ORDER, 1), jnp.float32)
    col_scale = 10.0 ** jax.random.uniform(key_cols, (1, ORDER), jnp.float32)
    values = jax.random.truncated_normal(key_vals, -4.0, 4.0, (ORDER, ORDER), jnp.float32)
    return values * row_scale * col_scale


def setup_inputs(seed: int = 0) -> dict:
    splits = jax.random.split(jax.random.key(seed), 2)
    return {
        "momentum": draw_momentum(jax.random.fold_in(splits[1], 71), 0),
    }


def reference(momentum):
    total = jnp.sum(momentum * momentum)
    scale = 1.0 / (jnp.sqrt(total) + 1e-07)
    tiles = (momentum * scale).astype(jnp.bfloat16)
    window = tiles[:, :WINDOW].astype(jnp.float32)
    gram = lax.dot_general(window, window, (((1,), (1,)), ((), ())), precision=lax.Precision.HIGHEST, preferred_element_type=jnp.float32)
    return (gram * jnp.float32(ORDER), tiles)
```

```python
import jax
import jax.numpy as jnp
from jax import lax
from jax.experimental import pallas as pl
from jax.experimental.pallas import tpu as pltpu
from jax.sharding import PartitionSpec as P

MESH = pl.DeviceIdType.MESH
BF16 = jnp.bfloat16
F32 = jnp.float32

COLS = 16
ROWS = 8
SHARD = 128
WIDTH = 1024
WINDOW = 2048
SUB = 64
MIB = 1 << 20
ISSUE = (2, 2, 2, 2, 2, 2, 2, 1)


def nothing(*_):
    return 0


def kernel(
    m_ref, gram_ref, tiles_ref,
    held, coded, panel, columns, sums1, sums2,
    load_sem, s1_send, s1_recv, s2_send, s2_recv,
    t_send, t_recv, r_send, r_recv, o_send, c_send, c_recv, local_sem,
):
    row = lax.axis_index("row")
    col = lax.axis_index("col")
    y, xh = row // 2, row % 2
    z, xl, core = col // 4, (col // 2) % 2, col % 2
    other = 1 - core
    up, down = (z + 1) % 4, (z + 3) % 4
    even = xh == xl
    turn = (y - z + 4) % 4
    home = turn == 0

    def place(y_, xh_, z_, xl_, core_):
        return (y_ * 2 + xh_, z_ * 4 + xl_ * 2 + core_)

    cross = place(y, 1 - xh, z, 1 - xl, core)

    def load(j):
        part = pl.ds(pl.multiple_of(j * 2 * WIDTH, 2 * WIDTH), 2 * WIDTH)
        return pltpu.make_async_copy(m_ref.at[:, part], held.at[:, part], load_sem.at[j])

    for j in range(8):
        load(j).start()

    barrier = pltpu.get_barrier_semaphore()

    def greet_col(i, _):
        pl.semaphore_signal(barrier, inc=1, device_id=(row, (col + i) % COLS), device_id_type=MESH)
        return 0

    def greet_row(i, _):
        pl.semaphore_signal(barrier, inc=1, device_id=((row + i) % ROWS, col), device_id_type=MESH)
        return 0

    lax.fori_loop(1, COLS, greet_col, 0)
    lax.fori_loop(1, ROWS, greet_row, 0)
    pl.semaphore_signal(barrier, inc=1, device_id=cross, device_id_type=MESH)

    def square(j, total):
        load(j).wait()
        part = held[:, pl.ds(pl.multiple_of(j * 2 * WIDTH, 2 * WIDTH), 2 * WIDTH)]
        part = (part * part).reshape(SHARD // 8, 8, 2 * WIDTH).sum(axis=0)
        for k in range(2 * WIDTH // 128):
            total = total + part[:, k * 128 : (k + 1) * 128]
        return total

    sums1[col] = lax.fori_loop(0, 8, square, jnp.zeros((8, 128), F32))

    pl.semaphore_wait(barrier, COLS + ROWS - 1)

    def send1(i):
        to = (col + i) % COLS
        return pltpu.make_async_remote_copy(
            src_ref=sums1.at[col], dst_ref=sums1.at[col], send_sem=s1_send.at[i], recv_sem=s1_recv.at[col],
            device_id=(row, to), device_id_type=MESH,
        )

    def recv1(i):
        source = (col + i) % COLS
        return pltpu.make_async_remote_copy(
            src_ref=sums1.at[source], dst_ref=sums1.at[source], send_sem=s1_send.at[i], recv_sem=s1_recv.at[source],
            device_id=(row, source), device_id_type=MESH,
        )

    def send2(i):
        to = (row + i) % ROWS
        return pltpu.make_async_remote_copy(
            src_ref=sums2.at[row], dst_ref=sums2.at[row], send_sem=s2_send.at[i], recv_sem=s2_recv.at[row],
            device_id=(to, col), device_id_type=MESH,
        )

    def recv2(i):
        source = (row + i) % ROWS
        return pltpu.make_async_remote_copy(
            src_ref=sums2.at[source], dst_ref=sums2.at[source], send_sem=s2_send.at[i], recv_sem=s2_recv.at[source],
            device_id=(source, col), device_id_type=MESH,
        )

    def each(low, high, act):
        def body(i, _):
            act(i)
            return 0

        lax.fori_loop(low, high, body, 0)

    each(1, COLS, lambda i: send1(i).start())
    each(1, COLS, lambda i: recv1(i).wait_recv())
    group = sums1[0]
    for k in range(1, COLS):
        group = group + sums1[k]
    sums2[row] = group
    each(1, ROWS, lambda i: send2(i).start())
    each(1, ROWS, lambda i: recv2(i).wait_recv())
    whole = sums2[0]
    for k in range(1, ROWS):
        whole = whole + sums2[k]
    total = jnp.sum(jnp.sum(whole, axis=0, keepdims=True), axis=1, keepdims=True)
    scale = 1.0 / (jnp.sqrt(total) + 1e-07)

    own = pl.multiple_of(col * SHARD, SHARD)
    panel[pl.ds(own, SHARD), :] = (held[:, :WINDOW] * scale).astype(BF16)

    def piece(block, s):
        return pl.ds(pl.multiple_of(block * SHARD + s * SUB, SUB), SUB)

    def pass_on(block, s, slot, target):
        return pltpu.make_async_remote_copy(
            src_ref=panel.at[piece(block, s)], dst_ref=panel.at[piece(block, s)],
            send_sem=r_send.at[slot, s], recv_sem=r_recv.at[block, s], device_id=target, device_id_type=MESH,
        )

    def arrived(block, s):
        pass_on(block, s, 0, (row, col)).wait_recv()

    def name(z_, xl_, core_):
        return z_ * 4 + xl_ * 2 + core_

    above = place(y, xh, up, xl, core)
    below = place(y, xh, down, xl, core)
    beside = place(y, xh, z, 1 - xl, core)
    sibling = place(y, xh, z, xl, other)

    def start_of(j):
        far = jnp.where(j < 6, 1, 3)
        return jnp.where(even | (j < 4), 0, far)

    def way_of(j):
        e = jnp.where(j < 4, 1, 3)
        m = jnp.where(j < 4, jnp.where(j < 2, 1, 3), jnp.where(j % 2 == 0, 1, 3))
        return jnp.where(even, e, m)

    def lead(block, s):
        j = block % 8
        near = (1 - xh, 1 - xl)
        step = jnp.where(even, way_of(j), start_of(j))
        direct = jnp.logical_not(even) & (j < 4)
        slot = jnp.where(even | (j < 4), j, 8 + j % 2)
        target = place(
            (y + step) % 4, jnp.where(direct, near[0], xh), z, jnp.where(direct, near[1], xl), core
        )
        return pltpu.make_async_remote_copy(
            src_ref=panel.at[piece(block, s)], dst_ref=columns.at[piece(slot, s)],
            send_sem=o_send.at[j, s], recv_sem=c_recv.at[slot, s], device_id=target, device_id_type=MESH,
        )

    def keep(block, s):
        return pltpu.make_async_copy(
            panel.at[piece(block, s)], columns.at[piece(block % 8, s)], local_sem.at[block % 8, s]
        )

    def have(block, s):
        @pl.when(home & (block // 8 == core))
        def _():
            lead(block, s).start()

            @pl.when(even)
            def _():
                keep(block, s).start()

    def tile_send(i):
        to = (col + i) % COLS
        return pltpu.make_async_remote_copy(
            src_ref=coded.at[to], dst_ref=tiles_ref.at[pl.ds(own, SHARD)],
            send_sem=t_send.at[i], recv_sem=t_recv.at[col], device_id=(row, to), device_id_type=MESH,
        )

    def tile_recv(i):
        source = (col + i) % COLS
        return pltpu.make_async_remote_copy(
            src_ref=coded.at[source], dst_ref=tiles_ref.at[pl.ds(pl.multiple_of(source * SHARD, SHARD), SHARD)],
            send_sem=t_send.at[i], recv_sem=t_recv.at[source], device_id=(row, source), device_id_type=MESH,
        )

    def tile_keep():
        return pltpu.make_async_copy(coded.at[col], tiles_ref.at[pl.ds(own, SHARD)], t_recv.at[col])

    def tile_start(i):
        @pl.when((col + i) % COLS >= 2)
        def _():
            tile_send(i).start()

    own_block = name(z, xl, core)

    def first(s):
        pass_on(own_block, s, 0, above).start()
        pass_on(own_block, s, 1, below).start()
        pass_on(own_block, s, 2, beside).start()
        pass_on(own_block, s, 3, sibling).start()
        have(own_block, s)

    each(0, 2, first)

    def code(t, _):
        part = held[:, pl.ds(pl.multiple_of(t * WIDTH, WIDTH), WIDTH)]
        coded[t] = (part * scale).astype(BF16)
        return 0

    lax.fori_loop(2, COLS, code, 0)

    steps = (
        (down, xl, (0, above, 4), None, 5),
        (up, xl, (1, below, 4), None, 6),
        (z, 1 - xl, None, ((above, 7), (below, 8)), 9),
        ((z + 2) % 4, xl, None, ((beside, 10),), 11),
        (down, 1 - xl, None, None, 12),
        (up, 1 - xl, None, None, 13),
        ((z + 2) % 4, 1 - xl, None, None, 14),
    )

    done = 1

    def issue(k):
        nonlocal done
        each(done, done + ISSUE[k], tile_start)
        done += ISSUE[k]

    issue(0)
    def sib_first(s):
        block = name(z, xl, other)
        arrived(block, s)
        have(block, s)

    each(0, 2, sib_first)
    for k, (z_, xl_, half, whole_sends, slot) in enumerate(steps):
        def at(s, z_=z_, xl_=xl_, half=half, whole_sends=whole_sends, slot=slot):
            block = name(z_, xl_, core)
            arrived(block, s)
            if half is not None:
                @pl.when(s == half[0])
                def _():
                    pass_on(block, s, half[2], half[1]).start()
            for target, n in whole_sends or ():
                pass_on(block, s, n, target).start()
            pass_on(block, s, slot, sibling).start()
            have(block, s)
            twin = name(z_, xl_, other)
            arrived(twin, s)
            have(twin, s)

        each(0, 2, at)
        issue(k + 1)

    def move(j, s, target):
        return pltpu.make_async_remote_copy(
            src_ref=columns.at[piece(j, s)], dst_ref=columns.at[piece(j, s)],
            send_sem=c_send.at[j, s], recv_sem=c_recv.at[j, s], device_id=target, device_id_type=MESH,
        )

    bridge = jnp.logical_not(even) & ((turn == 1) | (turn == 3))

    def relay(i, s):
        slot = jnp.where(turn == 1, 4, 6) + i
        return pltpu.make_async_remote_copy(
            src_ref=columns.at[piece(8 + i, s)], dst_ref=columns.at[piece(slot, s)],
            send_sem=c_send.at[8 + i, s], recv_sem=c_recv.at[slot, s], device_id=cross, device_id_type=MESH,
        )

    @pl.when(bridge)
    def _():
        def over(n):
            i, s = n // 2, n % 2
            move(8 + i, s, cross).wait_recv()
            relay(i, s).start()

        each(0, 4, over)

    def hop_of(j):
        ahead = (turn - start_of(j) + 4) % 4
        return jnp.where(way_of(j) == 1, ahead, (4 - ahead) % 4)

    def round_target(j):
        return place((y + way_of(j)) % 4, xh, z, xl, core)

    def carry(n):
        h, s, j = n // 16, (n // 8) % 2, n % 8

        @pl.when((hop_of(j) == h) & jnp.logical_not(even & (h == 0)))
        def _():
            move(j, s, cross).wait_recv()

            @pl.when(h < 3)
            def _():
                move(j, s, round_target(j)).start()

    each(0, 64, carry)

    @pl.when(home & even)
    def _():
        each(0, 16, lambda n: keep(core * 8 + n // 2, n % 2).wait())

    def multiply(n):
        i, k = n // 2, n % 2
        rows = pl.ds(pl.multiple_of(i * 512, 512), 512)
        cols = pl.ds(pl.multiple_of(k * 512, 512), 512)
        product = lax.dot_general(
            panel[rows, :], columns[cols, :], (((1,), (1,)), ((), ())), preferred_element_type=F32
        )
        gram_ref[rows, cols] = product * F32(WIDTH * COLS)

    each(0, 8, multiply)

    @pl.when(col >= 2)
    def _():
        tile_keep().start()
        each(1, COLS, lambda i: tile_recv(i).wait_recv())
        tile_keep().wait()

    @pl.when(col < 2)
    def _():
        def take(b):
            rows = pl.ds(pl.multiple_of(b * SHARD, SHARD), SHARD)
            tiles_ref[rows, :] = panel[rows, pl.ds(pl.multiple_of(core * WIDTH, WIDTH), WIDTH)]

        each(0, COLS, take)

    def left(i):
        @pl.when((col + i) % COLS >= 2)
        def _():
            tile_send(i).wait_send()

    each(1, COLS, left)
    each(1, COLS, lambda i: send1(i).wait_send())
    each(1, ROWS, lambda i: send2(i).wait_send())

    def gone(s):
        for n in range(15):
            pass_on(own_block, s, n, sibling).wait_send() if n != 4 else None

    each(0, 2, gone)
    pass_on(own_block, 0, 4, sibling).wait_send()
    pass_on(own_block, 1, 4, sibling).wait_send()

    @pl.when(home)
    def _():
        each(0, 16, lambda n: lead(core * 8 + n // 2, n % 2).wait_send())

    @pl.when(bridge)
    def _():
        each(0, 4, lambda n: relay(n // 2, n % 2).wait_send())

    def carried(n):
        s, j = n // 8, n % 8

        @pl.when((hop_of(j) < 3) & jnp.logical_not(even & home))
        def _():
            move(j, s, cross).wait_send()

    each(0, 16, carried)


def shards(momentum):
    dma = pltpu.SemaphoreType.DMA
    return pl.pallas_call(
        kernel,
        out_shape=(
            jax.ShapeDtypeStruct((COLS * SHARD, WIDTH), F32),
            jax.ShapeDtypeStruct((COLS * SHARD, WIDTH), BF16),
        ),
        in_specs=[pl.BlockSpec(memory_space=pltpu.HBM)],
        out_specs=(
            pl.BlockSpec(memory_space=pltpu.VMEM),
            pl.BlockSpec(memory_space=pltpu.VMEM),
        ),
        scratch_shapes=[
            pltpu.VMEM((SHARD, COLS * WIDTH), F32),
            pltpu.VMEM((COLS, SHARD, WIDTH), BF16),
            pltpu.VMEM((COLS * SHARD, WINDOW), BF16),
            pltpu.VMEM((10 * SHARD, WINDOW), BF16),
            pltpu.VMEM((COLS, 8, 128), F32),
            pltpu.VMEM((ROWS, 8, 128), F32),
            dma((8,)),
            dma((COLS,)),
            dma((COLS,)),
            dma((ROWS,)),
            dma((ROWS,)),
            dma((COLS,)),
            dma((COLS,)),
            dma((15, 2)),
            dma((COLS, 2)),
            dma((8, 2)),
            dma((10, 2)),
            dma((10, 2)),
            dma((8, 2)),
        ],
        compiler_params=pltpu.CompilerParams(
            collective_id=0, has_side_effects=True, vmem_limit_bytes=48 * MIB
        ),
        cost_estimate=pl.CostEstimate(
            flops=2 * COLS * SHARD * WIDTH * WINDOW, bytes_accessed=20 * MIB, transcendentals=0
        ),
        name="newton_gram",
    )(momentum)


def solution(mesh):
    return jax.shard_map(
        shards,
        mesh=mesh,
        in_specs=(P(("row", "col"), None),),
        out_specs=(P("row", "col"), P("row", "col")),
        check_vma=False,
    )
```

```python
import jax
import jax.numpy as jnp
from jax import lax
from jax.experimental import pallas as pl
from jax.experimental.pallas import tpu as pltpu
from jax.sharding import PartitionSpec as P

MESH = pl.DeviceIdType.MESH
BF16 = jnp.bfloat16
F32 = jnp.float32

COLS = 16
ROWS = 8
SHARD = 128
WIDTH = 1024
WINDOW = 2048
SUB = 64
MIB = 1 << 20
STEPS = 14
ISSUE = (0, 0, 0, 0, 0, 0, 15, 0, 0, 0, 0, 0, 0, 0)
PAIR = (0, 0, 1, 2, 1, 2, 3, 3)
TWIN = (0, 1, 0, 0, 1, 1, 0, 1)
READY = (2, 3, 4, 4, 5, 5, 6, 7)
RANK = ((0, 1), (2, 4), (3, 5), (6, 7))


def nothing(*_):
    return 0


def kernel(
    m_ref, gram_ref, tiles_ref,
    held, coded, panel, columns, sums1, sums2,
    load_sem, s1_send, s1_recv, s2_send, s2_recv,
    t_send, t_recv, r_send, r_recv, o_send, c_send, c_recv, local_sem,
):
    row = lax.axis_index("row")
    col = lax.axis_index("col")
    y, xh = row // 2, row % 2
    z, xl, core = col // 4, (col // 2) % 2, col % 2
    other = 1 - core
    up, down, opposite = (z + 1) % 4, (z + 3) % 4, (z + 2) % 4
    even = xh == xl
    turn = (y - z + 4) % 4
    home = turn == 0

    def place(y_, xh_, z_, xl_, core_):
        return (y_ * 2 + xh_, z_ * 4 + xl_ * 2 + core_)

    cross = place(y, 1 - xh, z, 1 - xl, core)

    def load(j):
        part = pl.ds(pl.multiple_of(j * 2 * WIDTH, 2 * WIDTH), 2 * WIDTH)
        return pltpu.make_async_copy(m_ref.at[:, part], held.at[:, part], load_sem.at[j])

    for j in range(8):
        load(j).start()

    barrier = pltpu.get_barrier_semaphore()

    def greet_col(i, _):
        pl.semaphore_signal(barrier, inc=1, device_id=(row, (col + i) % COLS), device_id_type=MESH)
        return 0

    def greet_row(i, _):
        pl.semaphore_signal(barrier, inc=1, device_id=((row + i) % ROWS, col), device_id_type=MESH)
        return 0

    lax.fori_loop(1, COLS, greet_col, 0)
    lax.fori_loop(1, ROWS, greet_row, 0)
    pl.semaphore_signal(barrier, inc=1, device_id=cross, device_id_type=MESH)

    def square(j, total):
        load(j).wait()
        part = held[:, pl.ds(pl.multiple_of(j * 2 * WIDTH, 2 * WIDTH), 2 * WIDTH)]
        part = (part * part).reshape(SHARD // 8, 8, 2 * WIDTH).sum(axis=0)
        for k in range(2 * WIDTH // 128):
            total = total + part[:, k * 128 : (k + 1) * 128]
        return total

    sums1[col] = lax.fori_loop(0, 8, square, jnp.zeros((8, 128), F32))

    pl.semaphore_wait(barrier, COLS + ROWS - 1)

    def send1(i):
        to = (col + i) % COLS
        return pltpu.make_async_remote_copy(
            src_ref=sums1.at[col], dst_ref=sums1.at[col], send_sem=s1_send.at[i], recv_sem=s1_recv.at[col],
            device_id=(row, to), device_id_type=MESH,
        )

    def recv1(i):
        source = (col + i) % COLS
        return pltpu.make_async_remote_copy(
            src_ref=sums1.at[source], dst_ref=sums1.at[source], send_sem=s1_send.at[i], recv_sem=s1_recv.at[source],
            device_id=(row, source), device_id_type=MESH,
        )

    def send2(i):
        to = (row + i) % ROWS
        return pltpu.make_async_remote_copy(
            src_ref=sums2.at[row], dst_ref=sums2.at[row], send_sem=s2_send.at[i], recv_sem=s2_recv.at[row],
            device_id=(to, col), device_id_type=MESH,
        )

    def recv2(i):
        source = (row + i) % ROWS
        return pltpu.make_async_remote_copy(
            src_ref=sums2.at[source], dst_ref=sums2.at[source], send_sem=s2_send.at[i], recv_sem=s2_recv.at[source],
            device_id=(source, col), device_id_type=MESH,
        )

    def each(low, high, act):
        def body(i, _):
            act(i)
            return 0

        lax.fori_loop(low, high, body, 0)

    each(1, COLS, lambda i: send1(i).start())
    each(1, COLS, lambda i: recv1(i).wait_recv())
    group = sums1[0]
    for k in range(1, COLS):
        group = group + sums1[k]
    sums2[row] = group
    each(1, ROWS, lambda i: send2(i).start())
    each(1, ROWS, lambda i: recv2(i).wait_recv())
    whole = sums2[0]
    for k in range(1, ROWS):
        whole = whole + sums2[k]
    total = jnp.sum(jnp.sum(whole, axis=0, keepdims=True), axis=1, keepdims=True)
    scale = 1.0 / (jnp.sqrt(total) + 1e-07)

    own = pl.multiple_of(col * SHARD, SHARD)
    panel[pl.ds(own, SHARD), :] = (held[:, :WINDOW] * scale).astype(BF16)

    def piece(block, s):
        return pl.ds(pl.multiple_of(block * SHARD + s * SUB, SUB), SUB)

    def pass_on(block, s, slot, target):
        return pltpu.make_async_remote_copy(
            src_ref=panel.at[piece(block, s)], dst_ref=panel.at[piece(block, s)],
            send_sem=r_send.at[slot, s], recv_sem=r_recv.at[block, s], device_id=target, device_id_type=MESH,
        )

    def arrived(block, s):
        pass_on(block, s, 0, (row, col)).wait_recv()

    def name(z_, xl_, core_):
        return z_ * 4 + xl_ * 2 + core_

    above = place(y, xh, up, xl, core)
    below = place(y, xh, down, xl, core)
    beside = place(y, xh, z, 1 - xl, core)
    sibling = place(y, xh, z, xl, other)

    def start_of(j):
        far = jnp.where(j % 4 == 0, 1, jnp.where(j % 4 == 1, 3, 0))
        return jnp.where(even, 0, far)

    def way_of(j):
        m = jnp.where(j % 4 < 2, jnp.where((j == 0) | (j == 5), 1, 3), jnp.where(j % 2 == 0, 1, 3))
        return jnp.where(even, jnp.where(j % 2 == 0, 1, 3), m)

    same = z // 2 == core
    near_z = jnp.where(same, z, opposite + 1 - 2 * (opposite % 2))
    far_z = jnp.where(same, z + 1 - 2 * (z % 2), opposite)

    def slot_of(j, holder_xl=xh):
        z_ = far_z if PAIR[j] % 2 else near_z
        xl_ = holder_xl if PAIR[j] < 2 else 1 - holder_xl
        return name(z_, xl_, other if TWIN[j] else core) % 8

    def lead(block, s, j):
        step = jnp.where(even, way_of(j), start_of(j))
        direct = jnp.logical_not(even) & (j % 4 >= 2)
        via = jnp.logical_not(even) & (j % 4 < 2)
        slot = jnp.where(via, 8 + j // 4, block % 8)
        sem = jnp.where(via, 8 + j // 4, j)
        target = place(
            (y + step) % 4, jnp.where(direct, 1 - xh, xh), z, jnp.where(direct, 1 - xl, xl), core
        )
        return pltpu.make_async_remote_copy(
            src_ref=panel.at[piece(block, s)], dst_ref=columns.at[piece(slot, s)],
            send_sem=o_send.at[j, s], recv_sem=c_recv.at[sem, s], device_id=target, device_id_type=MESH,
        )

    def keep(block, s):
        return pltpu.make_async_copy(
            panel.at[piece(block, s)], columns.at[piece(block % 8, s)], local_sem.at[block % 8, s]
        )

    def mine(z_):
        return home & (z_ // 2 == core)

    def have(z_, xl_, core_, s, beside_, twin):
        block = name(z_, xl_, core_)
        second = jnp.where(same, z_ != z, z_ == opposite)
        pair = 2 if beside_ else 0
        j = jnp.where(second, RANK[pair + 1][twin], RANK[pair][twin])

        @pl.when(mine(z_))
        def _():
            lead(block, s, j).start()

            @pl.when(even)
            def _():
                keep(block, s).start()

    def tile_send(i):
        to = (col + i) % COLS
        return pltpu.make_async_remote_copy(
            src_ref=coded.at[to], dst_ref=tiles_ref.at[pl.ds(own, SHARD)],
            send_sem=t_send.at[i], recv_sem=t_recv.at[col], device_id=(row, to), device_id_type=MESH,
        )

    def tile_recv(i):
        source = (col + i) % COLS
        return pltpu.make_async_remote_copy(
            src_ref=coded.at[source], dst_ref=tiles_ref.at[pl.ds(pl.multiple_of(source * SHARD, SHARD), SHARD)],
            send_sem=t_send.at[i], recv_sem=t_recv.at[source], device_id=(row, source), device_id_type=MESH,
        )

    def tile_keep():
        return pltpu.make_async_copy(coded.at[col], tiles_ref.at[pl.ds(own, SHARD)], t_recv.at[col])

    def tile_start(i):
        @pl.when((col + i) % COLS >= 2)
        def _():
            tile_send(i).start()

    own_block = name(z, xl, core)

    def first(s):
        pass_on(own_block, s, 0, above).start()
        pass_on(own_block, s, 1, below).start()
        pass_on(own_block, s, 2, beside).start()
        pass_on(own_block, s, 3, sibling).start()
        have(z, xl, core, s, False, 0)

    each(0, 2, first)

    def code(t, _):
        part = held[:, pl.ds(pl.multiple_of(t * WIDTH, WIDTH), WIDTH)]
        coded[t] = (part * scale).astype(BF16)
        return 0

    lax.fori_loop(2, COLS, code, 0)

    arrivals = (
        (1, down, xl, (0, above, 4), (), 5),
        (1, up, xl, (1, below, 4), (), 6),
        (1, z, 1 - xl, None, ((above, 7), (below, 8)), 9),
        (2, opposite, xl, None, ((beside, 10),), 11),
        (2, down, 1 - xl, None, (), 12),
        (2, up, 1 - xl, None, (), 13),
        (3, opposite, 1 - xl, None, (), 14),
    )

    def gather(z_, xl_, half, sends, slot, beside_):
        def at(s):
            block = name(z_, xl_, core)
            arrived(block, s)
            if half is not None:

                @pl.when(s == half[0])
                def _():
                    pass_on(block, s, half[2], half[1]).start()

            for target, n in sends:
                pass_on(block, s, n, target).start()
            pass_on(block, s, slot, sibling).start()
            have(z_, xl_, core, s, beside_, 0)

        each(0, 2, at)

    def from_sibling(z_, xl_, beside_):
        @pl.when(mine(z_))
        def _():
            def at(s):
                arrived(name(z_, xl_, other), s)
                have(z_, xl_, other, s, beside_, 1)

            each(0, 2, at)

    def move(slot, j, s, target):
        return pltpu.make_async_remote_copy(
            src_ref=columns.at[piece(slot, s)], dst_ref=columns.at[piece(slot, s)],
            send_sem=c_send.at[j, s], recv_sem=c_recv.at[j, s], device_id=target, device_id_type=MESH,
        )

    def bridge(j):
        return jnp.logical_not(even) & (turn == (3 if j % 4 else 1))

    def relay(j, s):
        slot = slot_of(j, 1 - xh)
        return pltpu.make_async_remote_copy(
            src_ref=columns.at[piece(8 + j // 4, s)], dst_ref=columns.at[piece(slot, s)],
            send_sem=c_send.at[8 + j // 4, s], recv_sem=c_recv.at[j, s], device_id=cross, device_id_type=MESH,
        )

    def hop_of(j):
        ahead = (turn - start_of(j) + 4) % 4
        return jnp.where(way_of(j) == 1, ahead, (4 - ahead) % 4)

    def round_target(j):
        return place((y + way_of(j)) % 4, xh, z, xl, core)

    def carry(step):
        for j in range(8):
            late = step - READY[j] + jnp.where(same, 2, 0)
            via = j % 4 < 2
            if via and 0 <= step - READY[j] <= 2:

                @pl.when(bridge(j) & (late == 2))
                def _(j=j):
                    def at(s):
                        move(8 + j // 4, 8 + j // 4, s, cross).wait_recv()
                        relay(j, s).start()

                    each(0, 2, at)

            if step - READY[j] in (0, 2, 4, 6, 8):
                hop = hop_of(j)
                begun = jnp.where(even, 0, 4 if via else 2)
                go = (late == begun + 2 * hop) & (hop < 3) & jnp.logical_not(even & home)

                @pl.when(go)
                def _(j=j):
                    def at(s):
                        move(slot_of(j), j, s, cross).wait_recv()
                        move(slot_of(j), j, s, round_target(j)).start()

                    each(0, 2, at)

    done = 1
    for step in range(STEPS):
        if step == 1:
            from_sibling(z, xl, False)
        for lv, z_, xl_, half, sends, slot in arrivals:
            if 2 * lv == step:
                gather(z_, xl_, half, sends, slot, xl_ is not xl)
        for lv, z_, xl_, half, sends, slot in arrivals:
            if 2 * lv + 1 == step:
                from_sibling(z_, xl_, xl_ is not xl)
        carry(step)
        each(done, done + ISSUE[step], tile_start)
        done += ISSUE[step]

    def last(j):
        @pl.when(hop_of(j) == 3)
        def _():
            def at(s):
                move(slot_of(j), j, s, cross).wait_recv()

            each(0, 2, at)

    def rest(n):
        block, s = n // 2, n % 2

        @pl.when((block % 2 == other) & jnp.logical_not(mine(block // 4)))
        def _():
            arrived(block, s)

    each(0, 2 * COLS, rest)

    @pl.when(home & even)
    def _():
        each(0, 16, lambda n: keep(core * 8 + n // 2, n % 2).wait())

    for pair in (0, 1, 2, 3):
        for j in range(8):
            if PAIR[j] == pair:
                last(j)
        first_slot = slot_of(PAIR.index(pair)) // 2 * 2
        rows = pl.ds(pl.multiple_of(first_slot * SHARD, 2 * SHARD), 2 * SHARD)

        def multiply(i, rows=rows):
            across = pl.ds(pl.multiple_of(i * 1024, 1024), 1024)
            product = lax.dot_general(
                panel[across, :], columns[rows, :], (((1,), (1,)), ((), ())), preferred_element_type=F32
            )
            gram_ref[across, rows] = product * F32(WIDTH * COLS)

        each(0, 2, multiply)

    @pl.when(col >= 2)
    def _():
        tile_keep().start()
        each(1, COLS, lambda i: tile_recv(i).wait_recv())
        tile_keep().wait()

    @pl.when(col < 2)
    def _():
        def take(b):
            rows = pl.ds(pl.multiple_of(b * SHARD, SHARD), SHARD)
            tiles_ref[rows, :] = panel[rows, pl.ds(pl.multiple_of(core * WIDTH, WIDTH), WIDTH)]

        each(0, COLS, take)

    def left(i):
        @pl.when((col + i) % COLS >= 2)
        def _():
            tile_send(i).wait_send()

    each(1, COLS, left)
    each(1, COLS, lambda i: send1(i).wait_send())
    each(1, ROWS, lambda i: send2(i).wait_send())

    def gone(s):
        for n in range(15):
            pass_on(own_block, s, n, sibling).wait_send() if n != 4 else None

    each(0, 2, gone)
    pass_on(own_block, 0, 4, sibling).wait_send()
    pass_on(own_block, 1, 4, sibling).wait_send()

    @pl.when(home)
    def _():
        each(0, 16, lambda n: lead(core * 8 + n // 2, n % 2, n // 2).wait_send())

    for j in range(8):
        if j % 4 < 2:

            @pl.when(bridge(j))
            def _(j=j):
                each(0, 2, lambda s: relay(j, s).wait_send())

        @pl.when((hop_of(j) < 3) & jnp.logical_not(even & home))
        def _(j=j):
            each(0, 2, lambda s: move(slot_of(j), j, s, cross).wait_send())


def shards(momentum):
    dma = pltpu.SemaphoreType.DMA
    return pl.pallas_call(
        kernel,
        out_shape=(
            pltpu.VMEM((COLS * SHARD, WIDTH), F32),
            pltpu.VMEM((COLS * SHARD, WIDTH), BF16),
        ),
        in_specs=[pl.BlockSpec(memory_space=pltpu.HBM)],
        out_specs=(
            pl.BlockSpec(memory_space=pltpu.VMEM),
            pl.BlockSpec(memory_space=pltpu.VMEM),
        ),
        scratch_shapes=[
            pltpu.VMEM((SHARD, COLS * WIDTH), F32),
            pltpu.VMEM((COLS, SHARD, WIDTH), BF16),
            pltpu.VMEM((COLS * SHARD, WINDOW), BF16),
            pltpu.VMEM((10 * SHARD, WINDOW), BF16),
            pltpu.VMEM((COLS, 8, 128), F32),
            pltpu.VMEM((ROWS, 8, 128), F32),
            dma((8,)),
            dma((COLS,)),
            dma((COLS,)),
            dma((ROWS,)),
            dma((ROWS,)),
            dma((COLS,)),
            dma((COLS,)),
            dma((15, 2)),
            dma((COLS, 2)),
            dma((8, 2)),
            dma((10, 2)),
            dma((10, 2)),
            dma((8, 2)),
        ],
        compiler_params=pltpu.CompilerParams(
            collective_id=0, has_side_effects=True, vmem_limit_bytes=36 * MIB
        ),
        cost_estimate=pl.CostEstimate(
            flops=2 * COLS * SHARD * WIDTH * WINDOW, bytes_accessed=20 * MIB, transcendentals=0
        ),
        name="newton_gram",
    )(momentum)


def solution(mesh):
    return jax.shard_map(
        shards,
        mesh=mesh,
        in_specs=(P(("row", "col"), None),),
        out_specs=(P("row", "col"), P("row", "col")),
        check_vma=False,
    )
```

```python
import jax
import jax.numpy as jnp
from jax import lax
from jax.experimental import pallas as pl
from jax.experimental.pallas import tpu as pltpu
from jax.sharding import PartitionSpec as P

MESH = pl.DeviceIdType.MESH
BF16 = jnp.bfloat16
F32 = jnp.float32

COLS = 16
ROWS = 8
SHARD = 128
WIDTH = 1024
WINDOW = 2048
PIECES = 4
SUB = SHARD // PIECES
MIB = 1 << 20
STEPS = 12
ISSUE = (0, 0, 0, 0, 0, 15, 0, 0, 0, 0, 0, 0)
TURNS = tuple(
    (dz, dx, dc)
    for dc in (0, 1)
    for dz, dx in ((1, 0), (3, 0), (0, 1), (2, 1), (1, 1), (3, 1), (2, 0), (0, 0))
    if (dz, dx, dc) != (0, 0, 0)
)
PAIR = (0, 0, 1, 2, 1, 2, 3, 3)
TWIN = (0, 1, 0, 0, 1, 1, 0, 1)
BASE = (3, 3, 5, 5, 7, 7, 8, 8)
RANK = ((0, 1), (2, 4), (3, 5), (6, 7))


def nothing(*_):
    return 0


def kernel(
    m_ref, gram_ref, tiles_ref,
    held, coded, panel, columns, sums1, sums2,
    load_sem, s1_send, s1_recv, s2_send, s2_recv,
    t_send, t_recv, r_send, r_recv, o_send, c_send, c_recv, local_sem,
):
    row = lax.axis_index("row")
    col = lax.axis_index("col")
    y, xh = row // 2, row % 2
    z, xl, core = col // 4, (col // 2) % 2, col % 2
    other = 1 - core
    up, down, opposite = (z + 1) % 4, (z + 3) % 4, (z + 2) % 4
    even = xh == xl
    turn = (y - z + 4) % 4
    home = turn == 0

    def place(y_, xh_, z_, xl_, core_):
        return (y_ * 2 + xh_, z_ * 4 + xl_ * 2 + core_)

    cross = place(y, 1 - xh, z, 1 - xl, core)

    def load(j):
        part = pl.ds(pl.multiple_of(j * 2 * WIDTH, 2 * WIDTH), 2 * WIDTH)
        return pltpu.make_async_copy(m_ref.at[:, part], held.at[:, part], load_sem.at[j])

    for j in range(8):
        load(j).start()

    barrier = pltpu.get_barrier_semaphore()

    def greet_col(i, _):
        pl.semaphore_signal(barrier, inc=1, device_id=(row, (col + i) % COLS), device_id_type=MESH)
        return 0

    def greet_row(i, _):
        pl.semaphore_signal(barrier, inc=1, device_id=((row + i) % ROWS, col), device_id_type=MESH)
        return 0

    lax.fori_loop(1, COLS, greet_col, 0)
    lax.fori_loop(1, ROWS, greet_row, 0)
    pl.semaphore_signal(barrier, inc=1, device_id=cross, device_id_type=MESH)

    def square(j, total):
        load(j).wait()
        part = held[:, pl.ds(pl.multiple_of(j * 2 * WIDTH, 2 * WIDTH), 2 * WIDTH)]
        part = (part * part).reshape(SHARD // 8, 8, 2 * WIDTH).sum(axis=0)
        for k in range(2 * WIDTH // 128):
            total = total + part[:, k * 128 : (k + 1) * 128]
        return total

    sums1[col] = lax.fori_loop(0, 8, square, jnp.zeros((8, 128), F32))

    pl.semaphore_wait(barrier, COLS + ROWS - 1)

    def send1(i):
        to = (col + i) % COLS
        return pltpu.make_async_remote_copy(
            src_ref=sums1.at[col], dst_ref=sums1.at[col], send_sem=s1_send.at[i], recv_sem=s1_recv.at[col],
            device_id=(row, to), device_id_type=MESH,
        )

    def recv1(i):
        source = (col + i) % COLS
        return pltpu.make_async_remote_copy(
            src_ref=sums1.at[source], dst_ref=sums1.at[source], send_sem=s1_send.at[i], recv_sem=s1_recv.at[source],
            device_id=(row, source), device_id_type=MESH,
        )

    def send2(i):
        to = (row + i) % ROWS
        return pltpu.make_async_remote_copy(
            src_ref=sums2.at[row], dst_ref=sums2.at[row], send_sem=s2_send.at[i], recv_sem=s2_recv.at[row],
            device_id=(to, col), device_id_type=MESH,
        )

    def recv2(i):
        source = (row + i) % ROWS
        return pltpu.make_async_remote_copy(
            src_ref=sums2.at[source], dst_ref=sums2.at[source], send_sem=s2_send.at[i], recv_sem=s2_recv.at[source],
            device_id=(source, col), device_id_type=MESH,
        )

    def each(low, high, act):
        def body(i, _):
            act(i)
            return 0

        lax.fori_loop(low, high, body, 0)

    each(1, COLS, lambda i: send1(i).start())
    each(1, COLS, lambda i: recv1(i).wait_recv())
    group = sums1[0]
    for k in range(1, COLS):
        group = group + sums1[k]
    sums2[row] = group
    each(1, ROWS, lambda i: send2(i).start())
    each(1, ROWS, lambda i: recv2(i).wait_recv())
    whole = sums2[0]
    for k in range(1, ROWS):
        whole = whole + sums2[k]
    total = jnp.sum(jnp.sum(whole, axis=0, keepdims=True), axis=1, keepdims=True)
    scale = 1.0 / (jnp.sqrt(total) + 1e-07)

    own = pl.multiple_of(col * SHARD, SHARD)
    panel[pl.ds(own, SHARD), :] = (held[:, :WINDOW] * scale).astype(BF16)

    def piece(block, s):
        return pl.ds(pl.multiple_of(block * SHARD + s * SUB, SUB), SUB)

    def pass_on(block, s, slot, target):
        return pltpu.make_async_remote_copy(
            src_ref=panel.at[piece(block, s)], dst_ref=panel.at[piece(block, s)],
            send_sem=r_send.at[slot, s], recv_sem=r_recv.at[block, s], device_id=target, device_id_type=MESH,
        )

    def arrived(block, s):
        pass_on(block, s, 0, (row, col)).wait_recv()

    def name(z_, xl_, core_):
        return z_ * 4 + xl_ * 2 + core_

    above = place(y, xh, up, xl, core)
    below = place(y, xh, down, xl, core)
    beside = place(y, xh, z, 1 - xl, core)
    sibling = place(y, xh, z, xl, other)

    def start_of(j):
        far = jnp.where(j % 4 == 0, 1, jnp.where(j % 4 == 1, 3, 0))
        return jnp.where(even, 0, far)

    def way_of(j):
        m = jnp.where(j % 4 < 2, jnp.where((j == 0) | (j == 5), 1, 3), jnp.where(j % 2 == 0, 1, 3))
        return jnp.where(even, jnp.where(j % 2 == 0, 1, 3), m)

    same = z // 2 == core
    near_z = jnp.where(same, z, opposite + 1 - 2 * (opposite % 2))
    far_z = jnp.where(same, z + 1 - 2 * (z % 2), opposite)

    def slot_of(j, holder_xl=xh):
        z_ = far_z if PAIR[j] % 2 else near_z
        xl_ = holder_xl if PAIR[j] < 2 else 1 - holder_xl
        return name(z_, xl_, other if TWIN[j] else core) % 8

    def lead(block, s, j):
        step = jnp.where(even, way_of(j), start_of(j))
        direct = jnp.logical_not(even) & (j % 4 >= 2)
        via = jnp.logical_not(even) & (j % 4 < 2)
        slot = jnp.where(via, 8 + j // 4, block % 8)
        sem = jnp.where(via, 8 + j // 4, j)
        target = place(
            (y + step) % 4, jnp.where(direct, 1 - xh, xh), z, jnp.where(direct, 1 - xl, xl), core
        )
        return pltpu.make_async_remote_copy(
            src_ref=panel.at[piece(block, s)], dst_ref=columns.at[piece(slot, s)],
            send_sem=o_send.at[j, s], recv_sem=c_recv.at[sem, s], device_id=target, device_id_type=MESH,
        )

    def keep(block, s):
        return pltpu.make_async_copy(
            panel.at[piece(block, s)], columns.at[piece(block % 8, s)], local_sem.at[block % 8, s]
        )

    def mine(z_):
        return home & (z_ // 2 == core)

    def have(z_, xl_, core_, s, beside_, twin):
        block = name(z_, xl_, core_)
        second = jnp.where(same, z_ != z, z_ == opposite)
        pair = 2 if beside_ else 0
        j = jnp.where(second, RANK[pair + 1][twin], RANK[pair][twin])

        @pl.when(mine(z_))
        def _():
            lead(block, s, j).start()

            @pl.when(even)
            def _():
                keep(block, s).start()

    def partner(i):
        dz, dx, dc = TURNS[i]
        return name((z + dz) % 4, 1 - xl if dx else xl, other if dc else core)

    def tile_send(i):
        to = partner(i)
        return pltpu.make_async_remote_copy(
            src_ref=coded.at[to], dst_ref=tiles_ref.at[pl.ds(own, SHARD)],
            send_sem=t_send.at[i], recv_sem=t_recv.at[col], device_id=(row, to), device_id_type=MESH,
        )

    def tile_recv(i):
        source = (col + i) % COLS
        return pltpu.make_async_remote_copy(
            src_ref=coded.at[source], dst_ref=tiles_ref.at[pl.ds(pl.multiple_of(source * SHARD, SHARD), SHARD)],
            send_sem=t_send.at[i], recv_sem=t_recv.at[source], device_id=(row, source), device_id_type=MESH,
        )

    def tile_keep():
        return pltpu.make_async_copy(coded.at[col], tiles_ref.at[pl.ds(own, SHARD)], t_recv.at[col])

    def tile_start(i):
        @pl.when(partner(i) >= 2)
        def _():
            tile_send(i).start()

    own_block = name(z, xl, core)

    def first(s):
        pass_on(own_block, s, 0, above).start()
        pass_on(own_block, s, 1, below).start()
        pass_on(own_block, s, 2, beside).start()
        pass_on(own_block, s, 3, sibling).start()
        have(z, xl, core, s, False, 0)

    each(0, PIECES, first)

    def code(t, _):
        part = held[:, pl.ds(pl.multiple_of(t * WIDTH, WIDTH), WIDTH)]
        coded[t] = (part * scale).astype(BF16)
        return 0

    lax.fori_loop(2, COLS, code, 0)

    arrivals = (
        (2, down, xl, (0, above, 4), (), 5),
        (2, up, xl, (1, below, 4), (), 6),
        (2, z, 1 - xl, None, ((above, 7), (below, 8)), 9),
        (4, opposite, xl, None, ((beside, 10),), 11),
        (5, down, 1 - xl, None, (), 12),
        (5, up, 1 - xl, None, (), 13),
        (6, opposite, 1 - xl, None, (), 14),
    )

    def gather(z_, xl_, half, sends, slot, beside_):
        def at(s):
            block = name(z_, xl_, core)
            arrived(block, s)
            if half is not None:

                @pl.when(s * 2 // PIECES == half[0])
                def _():
                    pass_on(block, s, half[2], half[1]).start()

            for target, n in sends:
                pass_on(block, s, n, target).start()
            pass_on(block, s, slot, sibling).start()
            have(z_, xl_, core, s, beside_, 0)

        each(0, PIECES, at)

    def from_sibling(z_, xl_, beside_):
        @pl.when(mine(z_))
        def _():
            def at(s):
                arrived(name(z_, xl_, other), s)
                have(z_, xl_, other, s, beside_, 1)

            each(0, PIECES, at)

    def move(slot, j, s, target):
        return pltpu.make_async_remote_copy(
            src_ref=columns.at[piece(slot, s)], dst_ref=columns.at[piece(slot, s)],
            send_sem=c_send.at[j, s], recv_sem=c_recv.at[j, s], device_id=target, device_id_type=MESH,
        )

    def bridge(j):
        return jnp.logical_not(even) & (turn == (3 if j % 4 else 1))

    def relay(j, s):
        slot = slot_of(j, 1 - xh)
        return pltpu.make_async_remote_copy(
            src_ref=columns.at[piece(8 + j // 4, s)], dst_ref=columns.at[piece(slot, s)],
            send_sem=c_send.at[8 + j // 4, s], recv_sem=c_recv.at[j, s], device_id=cross, device_id_type=MESH,
        )

    def hop_of(j):
        ahead = (turn - start_of(j) + 4) % 4
        return jnp.where(way_of(j) == 1, ahead, (4 - ahead) % 4)

    def round_target(j):
        return place((y + way_of(j)) % 4, xh, z, xl, core)

    def carry(step):
        for j in range(8):
            late = step - BASE[j] + jnp.where(same, 2, 0)
            via = j % 4 < 2
            if via and -1 <= step - BASE[j] <= 1:

                @pl.when(bridge(j) & (late == 1))
                def _(j=j):
                    def at(s):
                        move(8 + j // 4, 8 + j // 4, s, cross).wait_recv()
                        relay(j, s).start()

                    each(0, PIECES, at)

            if -1 <= step - BASE[j] <= (4 if via else 3):
                hop = hop_of(j)
                begun = jnp.where(even, 0, 2 if via else 1)
                go = (late == begun + hop) & (hop < 3) & jnp.logical_not(even & home)

                @pl.when(go)
                def _(j=j):
                    def at(s):
                        move(slot_of(j), j, s, cross).wait_recv()
                        move(slot_of(j), j, s, round_target(j)).start()

                    each(0, PIECES, at)

    def last(j):
        @pl.when(hop_of(j) == 3)
        def _():
            def at(s):
                move(slot_of(j), j, s, cross).wait_recv()

            each(0, PIECES, at)

    def product(pair):
        for j in range(8):
            if PAIR[j] == pair:
                last(j)
        first_slot = slot_of(PAIR.index(pair)) // 2 * 2
        rows = pl.ds(pl.multiple_of(first_slot * SHARD, 2 * SHARD), 2 * SHARD)

        def multiply(i):
            across = pl.ds(pl.multiple_of(i * 1024, 1024), 1024)
            block = lax.dot_general(
                panel[across, :], columns[rows, :], (((1,), (1,)), ((), ())), preferred_element_type=F32
            )
            gram_ref[across, rows] = block * F32(WIDTH * COLS)

        each(0, 2, multiply)

    done = 0
    for step in range(STEPS):
        if step == 1:
            from_sibling(z, xl, False)
        for at_step, z_, xl_, half, sends, slot in arrivals:
            if at_step == step:
                gather(z_, xl_, half, sends, slot, xl_ is not xl)
        for at_step, z_, xl_, half, sends, slot in arrivals:
            if at_step == step:
                from_sibling(z_, xl_, xl_ is not xl)
        carry(step)
        if step == 8:
            def rest(n):
                block, s = n // PIECES, n % PIECES

                @pl.when((block % 2 == other) & jnp.logical_not(mine(block // 4)))
                def _():
                    arrived(block, s)

            each(0, PIECES * COLS, rest)

            @pl.when(home & even)
            def _():
                each(0, 8 * PIECES, lambda n: keep(core * 8 + n // PIECES, n % PIECES).wait())
        if step == 9:
            product(0)
        for i in range(done, done + ISSUE[step]):
            tile_start(i)
        done += ISSUE[step]

    for pair in (1, 2, 3):
        product(pair)

    @pl.when(col >= 2)
    def _():
        tile_keep().start()
        each(1, COLS, lambda i: tile_recv(i).wait_recv())
        tile_keep().wait()

    @pl.when(col < 2)
    def _():
        def take(b):
            rows = pl.ds(pl.multiple_of(b * SHARD, SHARD), SHARD)
            tiles_ref[rows, :] = panel[rows, pl.ds(pl.multiple_of(core * WIDTH, WIDTH), WIDTH)]

        each(0, COLS, take)

    for i in range(len(TURNS)):

        @pl.when(partner(i) >= 2)
        def _(i=i):
            tile_send(i).wait_send()

    each(1, COLS, lambda i: send1(i).wait_send())
    each(1, ROWS, lambda i: send2(i).wait_send())

    def gone(s):
        for n in range(15):
            pass_on(own_block, s, n, sibling).wait_send()

    each(0, PIECES, gone)

    @pl.when(home)
    def _():
        each(0, 8 * PIECES, lambda n: lead(core * 8 + n // PIECES, n % PIECES, n // PIECES).wait_send())

    for j in range(8):
        if j % 4 < 2:

            @pl.when(bridge(j))
            def _(j=j):
                each(0, PIECES, lambda s: relay(j, s).wait_send())

        @pl.when((hop_of(j) < 3) & jnp.logical_not(even & home))
        def _(j=j):
            each(0, PIECES, lambda s: move(slot_of(j), j, s, cross).wait_send())


def shards(momentum):
    dma = pltpu.SemaphoreType.DMA
    return pl.pallas_call(
        kernel,
        out_shape=(
            pltpu.VMEM((COLS * SHARD, WIDTH), F32),
            pltpu.VMEM((COLS * SHARD, WIDTH), BF16),
        ),
        in_specs=[pl.BlockSpec(memory_space=pltpu.HBM)],
        out_specs=(
            pl.BlockSpec(memory_space=pltpu.VMEM),
            pl.BlockSpec(memory_space=pltpu.VMEM),
        ),
        scratch_shapes=[
            pltpu.VMEM((SHARD, COLS * WIDTH), F32),
            pltpu.VMEM((COLS, SHARD, WIDTH), BF16),
            pltpu.VMEM((COLS * SHARD, WINDOW), BF16),
            pltpu.VMEM((10 * SHARD, WINDOW), BF16),
            pltpu.VMEM((COLS, 8, 128), F32),
            pltpu.VMEM((ROWS, 8, 128), F32),
            dma((8,)),
            dma((COLS,)),
            dma((COLS,)),
            dma((ROWS,)),
            dma((ROWS,)),
            dma((COLS,)),
            dma((COLS,)),
            dma((15, PIECES)),
            dma((COLS, PIECES)),
            dma((8, PIECES)),
            dma((10, PIECES)),
            dma((10, PIECES)),
            dma((8, PIECES)),
        ],
        compiler_params=pltpu.CompilerParams(
            collective_id=0, has_side_effects=True, vmem_limit_bytes=36 * MIB
        ),
        cost_estimate=pl.CostEstimate(
            flops=2 * COLS * SHARD * WIDTH * WINDOW, bytes_accessed=20 * MIB, transcendentals=0
        ),
        name="newton_gram",
    )(momentum)


def solution(mesh):
    return jax.shard_map(
        shards,
        mesh=mesh,
        in_specs=(P(("row", "col"), None),),
        out_specs=(P("row", "col"), P("row", "col")),
        check_vma=False,
    )
```

```python
import jax
import jax.numpy as jnp
from jax import lax
from jax.experimental import pallas as pl
from jax.experimental.pallas import tpu as pltpu
from jax.sharding import PartitionSpec as P

MESH = pl.DeviceIdType.MESH
BF16 = jnp.bfloat16
F32 = jnp.float32

COLS = 16
ROWS = 8
SHARD = 128
WIDTH = 1024
WINDOW = 2048
PIECES = 4
SUB = SHARD // PIECES
MIB = 1 << 20
STEPS = 12
ISSUE = (0, 0, 0, 0, 0, 15, 0, 0, 0, 0, 0, 0)
TURNS = tuple(
    (dz, dx, dc)
    for dc in (0, 1)
    for dz, dx in ((1, 0), (3, 0), (0, 1), (2, 1), (1, 1), (3, 1), (2, 0), (0, 0))
    if (dz, dx, dc) != (0, 0, 0)
)
PAIR = (0, 0, 1, 2, 1, 2, 3, 3)
TWIN = (0, 1, 0, 0, 1, 1, 0, 1)
BASE = (3, 3, 5, 5, 7, 7, 8, 8)
RANK = ((0, 1), (2, 4), (3, 5), (6, 7))


def nothing(*_):
    return 0


def kernel(
    m_ref, gram_ref, tiles_ref,
    held, coded, panel, columns, sums1, sums2,
    load_sem, s1_send, s1_recv, s2_send, s2_recv,
    t_send, t_recv, r_send, r_recv, o_send, c_send, c_recv, local_sem,
):
    row = lax.axis_index("row")
    col = lax.axis_index("col")
    y, xh = row // 2, row % 2
    z, xl, core = col // 4, (col // 2) % 2, col % 2
    other = 1 - core
    up, down, opposite = (z + 1) % 4, (z + 3) % 4, (z + 2) % 4
    even = xh == xl
    turn = (y - z + 4) % 4
    home = turn == 0

    def place(y_, xh_, z_, xl_, core_):
        return (y_ * 2 + xh_, z_ * 4 + xl_ * 2 + core_)

    cross = place(y, 1 - xh, z, 1 - xl, core)

    def load(j):
        part = pl.ds(pl.multiple_of(j * 2 * WIDTH, 2 * WIDTH), 2 * WIDTH)
        return pltpu.make_async_copy(m_ref.at[:, part], held.at[:, part], load_sem.at[j])

    for j in range(8):
        load(j).start()

    barrier = pltpu.get_barrier_semaphore()

    def greet_col(i, _):
        pl.semaphore_signal(barrier, inc=1, device_id=(row, (col + i) % COLS), device_id_type=MESH)
        return 0

    def greet_row(i, _):
        pl.semaphore_signal(barrier, inc=1, device_id=((row + i) % ROWS, col), device_id_type=MESH)
        return 0

    lax.fori_loop(1, COLS, greet_col, 0)
    lax.fori_loop(1, ROWS, greet_row, 0)
    pl.semaphore_signal(barrier, inc=1, device_id=cross, device_id_type=MESH)

    def square(j, total):
        load(j).wait()
        part = held[:, pl.ds(pl.multiple_of(j * 2 * WIDTH, 2 * WIDTH), 2 * WIDTH)]
        part = (part * part).reshape(SHARD // 8, 8, 2 * WIDTH).sum(axis=0)
        for k in range(2 * WIDTH // 128):
            total = total + part[:, k * 128 : (k + 1) * 128]
        return total

    sums1[col] = lax.fori_loop(0, 8, square, jnp.zeros((8, 128), F32))

    pl.semaphore_wait(barrier, COLS + ROWS - 1)

    def send1(i):
        to = (col + i) % COLS
        return pltpu.make_async_remote_copy(
            src_ref=sums1.at[col], dst_ref=sums1.at[col], send_sem=s1_send.at[i], recv_sem=s1_recv.at[col],
            device_id=(row, to), device_id_type=MESH,
        )

    def recv1(i):
        source = (col + i) % COLS
        return pltpu.make_async_remote_copy(
            src_ref=sums1.at[source], dst_ref=sums1.at[source], send_sem=s1_send.at[i], recv_sem=s1_recv.at[source],
            device_id=(row, source), device_id_type=MESH,
        )

    def send2(i):
        to = (row + i) % ROWS
        return pltpu.make_async_remote_copy(
            src_ref=sums2.at[row], dst_ref=sums2.at[row], send_sem=s2_send.at[i], recv_sem=s2_recv.at[row],
            device_id=(to, col), device_id_type=MESH,
        )

    def recv2(i):
        source = (row + i) % ROWS
        return pltpu.make_async_remote_copy(
            src_ref=sums2.at[source], dst_ref=sums2.at[source], send_sem=s2_send.at[i], recv_sem=s2_recv.at[source],
            device_id=(source, col), device_id_type=MESH,
        )

    def each(low, high, act):
        def body(i, _):
            act(i)
            return 0

        lax.fori_loop(low, high, body, 0)

    each(1, COLS, lambda i: send1(i).start())
    each(1, COLS, lambda i: recv1(i).wait_recv())
    group = sums1[0]
    for k in range(1, COLS):
        group = group + sums1[k]
    sums2[row] = group
    each(1, ROWS, lambda i: send2(i).start())
    each(1, ROWS, lambda i: recv2(i).wait_recv())
    whole = sums2[0]
    for k in range(1, ROWS):
        whole = whole + sums2[k]
    total = jnp.sum(jnp.sum(whole, axis=0, keepdims=True), axis=1, keepdims=True)
    scale = 1.0 / (jnp.sqrt(total) + 1e-07)

    own = pl.multiple_of(col * SHARD, SHARD)
    panel[pl.ds(own, SHARD), :] = (held[:, :WINDOW] * scale).astype(BF16)

    def piece(block, s):
        return pl.ds(pl.multiple_of(block * SHARD + s * SUB, SUB), SUB)

    def pass_on(block, s, slot, target):
        return pltpu.make_async_remote_copy(
            src_ref=panel.at[piece(block, s)], dst_ref=panel.at[piece(block, s)],
            send_sem=r_send.at[slot, s], recv_sem=r_recv.at[block, s], device_id=target, device_id_type=MESH,
        )

    def arrived(block, s):
        pass_on(block, s, 0, (row, col)).wait_recv()

    def name(z_, xl_, core_):
        return z_ * 4 + xl_ * 2 + core_

    above = place(y, xh, up, xl, core)
    below = place(y, xh, down, xl, core)
    beside = place(y, xh, z, 1 - xl, core)
    sibling = place(y, xh, z, xl, other)

    def start_of(j):
        far = jnp.where(j % 4 == 0, 1, jnp.where(j % 4 == 1, 3, 0))
        return jnp.where(even, 0, far)

    def way_of(j):
        m = jnp.where(j % 4 < 2, jnp.where((j == 0) | (j == 5), 1, 3), jnp.where(j % 2 == 0, 1, 3))
        return jnp.where(even, jnp.where(j % 2 == 0, 1, 3), m)

    same = z // 2 == core
    near_z = jnp.where(same, z, opposite + 1 - 2 * (opposite % 2))
    far_z = jnp.where(same, z + 1 - 2 * (z % 2), opposite)

    def slot_of(j, holder_xl=xh):
        z_ = far_z if PAIR[j] % 2 else near_z
        xl_ = holder_xl if PAIR[j] < 2 else 1 - holder_xl
        return name(z_, xl_, other if TWIN[j] else core) % 8

    def lead(block, s, j):
        step = jnp.where(even, way_of(j), start_of(j))
        direct = jnp.logical_not(even) & (j % 4 >= 2)
        via = jnp.logical_not(even) & (j % 4 < 2)
        slot = jnp.where(via, 8 + j // 4, block % 8)
        sem = jnp.where(via, 8 + j // 4, j)
        target = place(
            (y + step) % 4, jnp.where(direct, 1 - xh, xh), z, jnp.where(direct, 1 - xl, xl), core
        )
        return pltpu.make_async_remote_copy(
            src_ref=panel.at[piece(block, s)], dst_ref=columns.at[piece(slot, s)],
            send_sem=o_send.at[j, s], recv_sem=c_recv.at[sem, s], device_id=target, device_id_type=MESH,
        )

    def keep(block, s):
        return pltpu.make_async_copy(
            panel.at[piece(block, s)], columns.at[piece(block % 8, s)], local_sem.at[block % 8, s]
        )

    def mine(z_):
        return home & (z_ // 2 == core)

    def have(z_, xl_, core_, s, beside_, twin):
        block = name(z_, xl_, core_)
        second = jnp.where(same, z_ != z, z_ == opposite)
        pair = 2 if beside_ else 0
        j = jnp.where(second, RANK[pair + 1][twin], RANK[pair][twin])

        @pl.when(mine(z_))
        def _():
            lead(block, s, j).start()

            @pl.when(even)
            def _():
                keep(block, s).start()

    def partner(i):
        dz, dx, dc = TURNS[i]
        return name((z + dz) % 4, 1 - xl if dx else xl, other if dc else core)

    def tile_send(i):
        to = partner(i)
        return pltpu.make_async_remote_copy(
            src_ref=coded.at[to], dst_ref=tiles_ref.at[pl.ds(own, SHARD)],
            send_sem=t_send.at[i], recv_sem=t_recv.at[col], device_id=(row, to), device_id_type=MESH,
        )

    def tile_recv(i):
        source = (col + i) % COLS
        return pltpu.make_async_remote_copy(
            src_ref=coded.at[source], dst_ref=tiles_ref.at[pl.ds(pl.multiple_of(source * SHARD, SHARD), SHARD)],
            send_sem=t_send.at[i], recv_sem=t_recv.at[source], device_id=(row, source), device_id_type=MESH,
        )

    def tile_keep():
        return pltpu.make_async_copy(coded.at[col], tiles_ref.at[pl.ds(own, SHARD)], t_recv.at[col])

    def tile_start(i):
        @pl.when(partner(i) >= 2)
        def _():
            tile_send(i).start()

    own_block = name(z, xl, core)

    def first(s):
        pass_on(own_block, s, 0, above).start()
        pass_on(own_block, s, 1, below).start()
        pass_on(own_block, s, 2, beside).start()
        pass_on(own_block, s, 3, sibling).start()
        have(z, xl, core, s, False, 0)

    each(0, PIECES, first)

    arrivals = (
        (2, down, xl, (0, above, 4), (), 5),
        (2, up, xl, (1, below, 4), (), 6),
        (2, z, 1 - xl, None, ((above, 7), (below, 8)), 9),
        (4, opposite, xl, None, ((beside, 10),), 11),
        (5, down, 1 - xl, None, (), 12),
        (5, up, 1 - xl, None, (), 13),
        (6, opposite, 1 - xl, None, (), 14),
    )

    def gather(z_, xl_, half, sends, slot, beside_):
        def at(s):
            block = name(z_, xl_, core)
            arrived(block, s)
            if half is not None:

                @pl.when(s * 2 // PIECES == half[0])
                def _():
                    pass_on(block, s, half[2], half[1]).start()

            for target, n in sends:
                pass_on(block, s, n, target).start()
            pass_on(block, s, slot, sibling).start()
            have(z_, xl_, core, s, beside_, 0)

        each(0, PIECES, at)

    def from_sibling(z_, xl_, beside_):
        @pl.when(mine(z_))
        def _():
            def at(s):
                arrived(name(z_, xl_, other), s)
                have(z_, xl_, other, s, beside_, 1)

            each(0, PIECES, at)

    def move(slot, j, s, target):
        return pltpu.make_async_remote_copy(
            src_ref=columns.at[piece(slot, s)], dst_ref=columns.at[piece(slot, s)],
            send_sem=c_send.at[j, s], recv_sem=c_recv.at[j, s], device_id=target, device_id_type=MESH,
        )

    def bridge(j):
        return jnp.logical_not(even) & (turn == (3 if j % 4 else 1))

    def relay(j, s):
        slot = slot_of(j, 1 - xh)
        return pltpu.make_async_remote_copy(
            src_ref=columns.at[piece(8 + j // 4, s)], dst_ref=columns.at[piece(slot, s)],
            send_sem=c_send.at[8 + j // 4, s], recv_sem=c_recv.at[j, s], device_id=cross, device_id_type=MESH,
        )

    def hop_of(j):
        ahead = (turn - start_of(j) + 4) % 4
        return jnp.where(way_of(j) == 1, ahead, (4 - ahead) % 4)

    def round_target(j):
        return place((y + way_of(j)) % 4, xh, z, xl, core)

    def carry(step):
        for j in range(8):
            late = step - BASE[j] + jnp.where(same, 2, 0)
            via = j % 4 < 2
            if via and -1 <= step - BASE[j] <= 1:

                @pl.when(bridge(j) & (late == 1))
                def _(j=j):
                    def at(s):
                        move(8 + j // 4, 8 + j // 4, s, cross).wait_recv()
                        relay(j, s).start()

                    each(0, PIECES, at)

            if -1 <= step - BASE[j] <= (4 if via else 3):
                hop = hop_of(j)
                begun = jnp.where(even, 0, 2 if via else 1)
                go = (late == begun + hop) & (hop < 3) & jnp.logical_not(even & home)

                @pl.when(go)
                def _(j=j):
                    def at(s):
                        move(slot_of(j), j, s, cross).wait_recv()
                        move(slot_of(j), j, s, round_target(j)).start()

                    each(0, PIECES, at)

    def last(j):
        @pl.when(hop_of(j) == 3)
        def _():
            def at(s):
                move(slot_of(j), j, s, cross).wait_recv()

            each(0, PIECES, at)

    def product(pair):
        for j in range(8):
            if PAIR[j] == pair:
                last(j)
        first_slot = slot_of(PAIR.index(pair)) // 2 * 2
        rows = pl.ds(pl.multiple_of(first_slot * SHARD, 2 * SHARD), 2 * SHARD)

        def multiply(i):
            across = pl.ds(pl.multiple_of(i * 1024, 1024), 1024)
            block = lax.dot_general(
                panel[across, :], columns[rows, :], (((1,), (1,)), ((), ())), preferred_element_type=F32
            )
            gram_ref[across, rows] = block * F32(WIDTH * COLS)

        each(0, 2, multiply)

    def code(t, _):
        part = held[:, pl.ds(pl.multiple_of(t * WIDTH, WIDTH), WIDTH)]
        coded[t] = (part * scale).astype(BF16)
        return 0

    done = 0
    for step in range(STEPS):
        if step == 1:
            from_sibling(z, xl, False)
        for at_step, z_, xl_, half, sends, slot in arrivals:
            if at_step == step:
                gather(z_, xl_, half, sends, slot, xl_ is not xl)
        for at_step, z_, xl_, half, sends, slot in arrivals:
            if at_step == step:
                from_sibling(z_, xl_, xl_ is not xl)
        carry(step)
        if step == 2:
            lax.fori_loop(2, COLS, code, 0)
        if step == 8:
            def rest(n):
                block, s = n // PIECES, n % PIECES

                @pl.when((block % 2 == other) & jnp.logical_not(mine(block // 4)))
                def _():
                    arrived(block, s)

            each(0, PIECES * COLS, rest)

            @pl.when(home & even)
            def _():
                each(0, 8 * PIECES, lambda n: keep(core * 8 + n // PIECES, n % PIECES).wait())
        for i in range(done, done + ISSUE[step]):
            tile_start(i)
        done += ISSUE[step]

    for pair in (0, 1, 2, 3):
        product(pair)

    @pl.when(col >= 2)
    def _():
        tile_keep().start()
        each(1, COLS, lambda i: tile_recv(i).wait_recv())
        tile_keep().wait()

    @pl.when(col < 2)
    def _():
        def take(b):
            rows = pl.ds(pl.multiple_of(b * SHARD, SHARD), SHARD)
            tiles_ref[rows, :] = panel[rows, pl.ds(pl.multiple_of(core * WIDTH, WIDTH), WIDTH)]

        each(0, COLS, take)

    for i in range(len(TURNS)):

        @pl.when(partner(i) >= 2)
        def _(i=i):
            tile_send(i).wait_send()

    each(1, COLS, lambda i: send1(i).wait_send())
    each(1, ROWS, lambda i: send2(i).wait_send())

    def gone(s):
        for n in range(15):
            pass_on(own_block, s, n, sibling).wait_send()

    each(0, PIECES, gone)

    @pl.when(home)
    def _():
        each(0, 8 * PIECES, lambda n: lead(core * 8 + n // PIECES, n % PIECES, n // PIECES).wait_send())

    for j in range(8):
        if j % 4 < 2:

            @pl.when(bridge(j))
            def _(j=j):
                each(0, PIECES, lambda s: relay(j, s).wait_send())

        @pl.when((hop_of(j) < 3) & jnp.logical_not(even & home))
        def _(j=j):
            each(0, PIECES, lambda s: move(slot_of(j), j, s, cross).wait_send())


def shards(momentum):
    dma = pltpu.SemaphoreType.DMA
    return pl.pallas_call(
        kernel,
        out_shape=(
            pltpu.VMEM((COLS * SHARD, WIDTH), F32),
            pltpu.VMEM((COLS * SHARD, WIDTH), BF16),
        ),
        in_specs=[pl.BlockSpec(memory_space=pltpu.HBM)],
        out_specs=(
            pl.BlockSpec(memory_space=pltpu.VMEM),
            pl.BlockSpec(memory_space=pltpu.VMEM),
        ),
        scratch_shapes=[
            pltpu.VMEM((SHARD, COLS * WIDTH), F32),
            pltpu.VMEM((COLS, SHARD, WIDTH), BF16),
            pltpu.VMEM((COLS * SHARD, WINDOW), BF16),
            pltpu.VMEM((10 * SHARD, WINDOW), BF16),
            pltpu.VMEM((COLS, 8, 128), F32),
            pltpu.VMEM((ROWS, 8, 128), F32),
            dma((8,)),
            dma((COLS,)),
            dma((COLS,)),
            dma((ROWS,)),
            dma((ROWS,)),
            dma((COLS,)),
            dma((COLS,)),
            dma((15, PIECES)),
            dma((COLS, PIECES)),
            dma((8, PIECES)),
            dma((10, PIECES)),
            dma((10, PIECES)),
            dma((8, PIECES)),
        ],
        compiler_params=pltpu.CompilerParams(
            collective_id=0, has_side_effects=True, vmem_limit_bytes=36 * MIB
        ),
        cost_estimate=pl.CostEstimate(
            flops=2 * COLS * SHARD * WIDTH * WINDOW, bytes_accessed=20 * MIB, transcendentals=0
        ),
        name="newton_gram",
    )(momentum)


def solution(mesh):
    return jax.shard_map(
        shards,
        mesh=mesh,
        in_specs=(P(("row", "col"), None),),
        out_specs=(P("row", "col"), P("row", "col")),
        check_vma=False,
    )
```

```python
import jax
import jax.numpy as jnp
from jax import lax
from jax.experimental import pallas as pl
from jax.experimental.pallas import tpu as pltpu
from jax.sharding import PartitionSpec as P

MESH = pl.DeviceIdType.MESH
BF16 = jnp.bfloat16
F32 = jnp.float32

COLS = 16
ROWS = 8
SHARD = 128
WIDTH = 1024
WINDOW = 2048
PIECES = 4
SUB = SHARD // PIECES
MIB = 1 << 20
STEPS = 12
ISSUE = (0, 0, 0, 0, 0, 7, 8, 0, 0, 0, 0, 0)
TURNS = tuple(
    (dz, dx, dc)
    for dx in (0, 1)
    for dc in (0, 1)
    for dz in (1, 3, 2, 0)
    if (dz, dx, dc) != (0, 0, 0)
)
PAIR = (0, 0, 1, 2, 1, 2, 3, 3)
TWIN = (0, 1, 0, 0, 1, 1, 0, 1)
BASE = (3, 3, 5, 5, 7, 7, 8, 8)
RANK = ((0, 1), (2, 4), (3, 5), (6, 7))


def nothing(*_):
    return 0


def kernel(
    m_ref, gram_ref, tiles_ref,
    held, coded, panel, columns, sums1, sums2,
    load_sem, s1_send, s1_recv, s2_send, s2_recv,
    t_send, t_recv, r_send, r_recv, o_send, c_send, c_recv, local_sem,
):
    row = lax.axis_index("row")
    col = lax.axis_index("col")
    y, xh = row // 2, row % 2
    z, xl, core = col // 4, (col // 2) % 2, col % 2
    other = 1 - core
    up, down, opposite = (z + 1) % 4, (z + 3) % 4, (z + 2) % 4
    even = xh == xl
    turn = (y - z + 4) % 4
    home = turn == 0

    def place(y_, xh_, z_, xl_, core_):
        return (y_ * 2 + xh_, z_ * 4 + xl_ * 2 + core_)

    cross = place(y, 1 - xh, z, 1 - xl, core)

    def load(j):
        part = pl.ds(pl.multiple_of(j * 2 * WIDTH, 2 * WIDTH), 2 * WIDTH)
        return pltpu.make_async_copy(m_ref.at[:, part], held.at[:, part], load_sem.at[j])

    for j in range(8):
        load(j).start()

    barrier = pltpu.get_barrier_semaphore()

    def greet_col(i, _):
        pl.semaphore_signal(barrier, inc=1, device_id=(row, (col + i) % COLS), device_id_type=MESH)
        return 0

    def greet_row(i, _):
        pl.semaphore_signal(barrier, inc=1, device_id=((row + i) % ROWS, col), device_id_type=MESH)
        return 0

    lax.fori_loop(1, COLS, greet_col, 0)
    lax.fori_loop(1, ROWS, greet_row, 0)
    pl.semaphore_signal(barrier, inc=1, device_id=cross, device_id_type=MESH)

    def square(j, total):
        load(j).wait()
        part = held[:, pl.ds(pl.multiple_of(j * 2 * WIDTH, 2 * WIDTH), 2 * WIDTH)]
        part = (part * part).reshape(SHARD // 8, 8, 2 * WIDTH).sum(axis=0)
        for k in range(2 * WIDTH // 128):
            total = total + part[:, k * 128 : (k + 1) * 128]
        return total

    sums1[col] = lax.fori_loop(0, 8, square, jnp.zeros((8, 128), F32))

    pl.semaphore_wait(barrier, COLS + ROWS - 1)

    def send1(i):
        to = (col + i) % COLS
        return pltpu.make_async_remote_copy(
            src_ref=sums1.at[col], dst_ref=sums1.at[col], send_sem=s1_send.at[i], recv_sem=s1_recv.at[col],
            device_id=(row, to), device_id_type=MESH,
        )

    def recv1(i):
        source = (col + i) % COLS
        return pltpu.make_async_remote_copy(
            src_ref=sums1.at[source], dst_ref=sums1.at[source], send_sem=s1_send.at[i], recv_sem=s1_recv.at[source],
            device_id=(row, source), device_id_type=MESH,
        )

    def send2(i):
        to = (row + i) % ROWS
        return pltpu.make_async_remote_copy(
            src_ref=sums2.at[row], dst_ref=sums2.at[row], send_sem=s2_send.at[i], recv_sem=s2_recv.at[row],
            device_id=(to, col), device_id_type=MESH,
        )

    def recv2(i):
        source = (row + i) % ROWS
        return pltpu.make_async_remote_copy(
            src_ref=sums2.at[source], dst_ref=sums2.at[source], send_sem=s2_send.at[i], recv_sem=s2_recv.at[source],
            device_id=(source, col), device_id_type=MESH,
        )

    def each(low, high, act):
        def body(i, _):
            act(i)
            return 0

        lax.fori_loop(low, high, body, 0)

    each(1, COLS, lambda i: send1(i).start())
    each(1, COLS, lambda i: recv1(i).wait_recv())
    group = sums1[0]
    for k in range(1, COLS):
        group = group + sums1[k]
    sums2[row] = group
    each(1, ROWS, lambda i: send2(i).start())
    each(1, ROWS, lambda i: recv2(i).wait_recv())
    whole = sums2[0]
    for k in range(1, ROWS):
        whole = whole + sums2[k]
    total = jnp.sum(jnp.sum(whole, axis=0, keepdims=True), axis=1, keepdims=True)
    scale = 1.0 / (jnp.sqrt(total) + 1e-07)

    own = pl.multiple_of(col * SHARD, SHARD)
    panel[pl.ds(own, SHARD), :] = (held[:, :WINDOW] * scale).astype(BF16)

    def piece(block, s):
        return pl.ds(pl.multiple_of(block * SHARD + s * SUB, SUB), SUB)

    def pass_on(block, s, slot, target):
        return pltpu.make_async_remote_copy(
            src_ref=panel.at[piece(block, s)], dst_ref=panel.at[piece(block, s)],
            send_sem=r_send.at[slot, s], recv_sem=r_recv.at[block, s], device_id=target, device_id_type=MESH,
        )

    def arrived(block, s):
        pass_on(block, s, 0, (row, col)).wait_recv()

    def name(z_, xl_, core_):
        return z_ * 4 + xl_ * 2 + core_

    above = place(y, xh, up, xl, core)
    below = place(y, xh, down, xl, core)
    beside = place(y, xh, z, 1 - xl, core)
    sibling = place(y, xh, z, xl, other)

    def start_of(j):
        far = jnp.where(j % 4 == 0, 1, jnp.where(j % 4 == 1, 3, 0))
        return jnp.where(even, 0, far)

    def way_of(j):
        m = jnp.where(j % 4 < 2, jnp.where((j == 0) | (j == 5), 1, 3), jnp.where(j % 2 == 0, 1, 3))
        return jnp.where(even, jnp.where(j % 2 == 0, 1, 3), m)

    same = z // 2 == core
    near_z = jnp.where(same, z, opposite + 1 - 2 * (opposite % 2))
    far_z = jnp.where(same, z + 1 - 2 * (z % 2), opposite)

    def slot_of(j, holder_xl=xh):
        z_ = far_z if PAIR[j] % 2 else near_z
        xl_ = holder_xl if PAIR[j] < 2 else 1 - holder_xl
        return name(z_, xl_, other if TWIN[j] else core) % 8

    def lead(block, s, j):
        step = jnp.where(even, way_of(j), start_of(j))
        direct = jnp.logical_not(even) & (j % 4 >= 2)
        via = jnp.logical_not(even) & (j % 4 < 2)
        slot = jnp.where(via, 8 + j // 4, block % 8)
        sem = jnp.where(via, 8 + j // 4, j)
        target = place(
            (y + step) % 4, jnp.where(direct, 1 - xh, xh), z, jnp.where(direct, 1 - xl, xl), core
        )
        return pltpu.make_async_remote_copy(
            src_ref=panel.at[piece(block, s)], dst_ref=columns.at[piece(slot, s)],
            send_sem=o_send.at[j, s], recv_sem=c_recv.at[sem, s], device_id=target, device_id_type=MESH,
        )

    def keep(block, s):
        return pltpu.make_async_copy(
            panel.at[piece(block, s)], columns.at[piece(block % 8, s)], local_sem.at[block % 8, s]
        )

    def mine(z_):
        return home & (z_ // 2 == core)

    def have(z_, xl_, core_, s, beside_, twin):
        block = name(z_, xl_, core_)
        second = jnp.where(same, z_ != z, z_ == opposite)
        pair = 2 if beside_ else 0
        j = jnp.where(second, RANK[pair + 1][twin], RANK[pair][twin])

        @pl.when(mine(z_))
        def _():
            lead(block, s, j).start()

            @pl.when(even)
            def _():
                keep(block, s).start()

    def partner(i):
        dz, dx, dc = TURNS[i]
        return name((z + dz) % 4, 1 - xl if dx else xl, other if dc else core)

    def tile_send(i):
        to = partner(i)
        return pltpu.make_async_remote_copy(
            src_ref=coded.at[to], dst_ref=tiles_ref.at[pl.ds(own, SHARD)],
            send_sem=t_send.at[i], recv_sem=t_recv.at[col], device_id=(row, to), device_id_type=MESH,
        )

    def tile_recv(i):
        source = (col + i) % COLS
        return pltpu.make_async_remote_copy(
            src_ref=coded.at[source], dst_ref=tiles_ref.at[pl.ds(pl.multiple_of(source * SHARD, SHARD), SHARD)],
            send_sem=t_send.at[i], recv_sem=t_recv.at[source], device_id=(row, source), device_id_type=MESH,
        )

    def tile_keep():
        return pltpu.make_async_copy(coded.at[col], tiles_ref.at[pl.ds(own, SHARD)], t_recv.at[col])

    def tile_start(i):
        @pl.when(partner(i) >= 2)
        def _():
            tile_send(i).start()

    own_block = name(z, xl, core)

    def first(s):
        pass_on(own_block, s, 0, above).start()
        pass_on(own_block, s, 1, below).start()
        pass_on(own_block, s, 2, beside).start()
        pass_on(own_block, s, 3, sibling).start()
        have(z, xl, core, s, False, 0)

    each(0, PIECES, first)

    arrivals = (
        (2, down, xl, (0, above, 4), (), 5),
        (2, up, xl, (1, below, 4), (), 6),
        (2, z, 1 - xl, None, ((above, 7), (below, 8)), 9),
        (4, opposite, xl, None, ((beside, 10),), 11),
        (5, down, 1 - xl, None, (), 12),
        (5, up, 1 - xl, None, (), 13),
        (6, opposite, 1 - xl, None, (), 14),
    )

    def gather(z_, xl_, half, sends, slot, beside_):
        def at(s):
            block = name(z_, xl_, core)
            arrived(block, s)
            if half is not None:

                @pl.when(s * 2 // PIECES == half[0])
                def _():
                    pass_on(block, s, half[2], half[1]).start()

            for target, n in sends:
                pass_on(block, s, n, target).start()
            pass_on(block, s, slot, sibling).start()
            have(z_, xl_, core, s, beside_, 0)

        each(0, PIECES, at)

    def from_sibling(z_, xl_, beside_):
        @pl.when(mine(z_))
        def _():
            def at(s):
                arrived(name(z_, xl_, other), s)
                have(z_, xl_, other, s, beside_, 1)

            each(0, PIECES, at)

    def move(slot, j, s, target):
        return pltpu.make_async_remote_copy(
            src_ref=columns.at[piece(slot, s)], dst_ref=columns.at[piece(slot, s)],
            send_sem=c_send.at[j, s], recv_sem=c_recv.at[j, s], device_id=target, device_id_type=MESH,
        )

    def bridge(j):
        return jnp.logical_not(even) & (turn == (3 if j % 4 else 1))

    def relay(j, s):
        slot = slot_of(j, 1 - xh)
        return pltpu.make_async_remote_copy(
            src_ref=columns.at[piece(8 + j // 4, s)], dst_ref=columns.at[piece(slot, s)],
            send_sem=c_send.at[8 + j // 4, s], recv_sem=c_recv.at[j, s], device_id=cross, device_id_type=MESH,
        )

    def hop_of(j):
        ahead = (turn - start_of(j) + 4) % 4
        return jnp.where(way_of(j) == 1, ahead, (4 - ahead) % 4)

    def round_target(j):
        return place((y + way_of(j)) % 4, xh, z, xl, core)

    def carry(step):
        for j in range(8):
            late = step - BASE[j] + jnp.where(same, 2, 0)
            via = j % 4 < 2
            if via and -1 <= step - BASE[j] <= 1:

                @pl.when(bridge(j) & (late == 1))
                def _(j=j):
                    def at(s):
                        move(8 + j // 4, 8 + j // 4, s, cross).wait_recv()
                        relay(j, s).start()

                    each(0, PIECES, at)

            if -1 <= step - BASE[j] <= (4 if via else 3):
                hop = hop_of(j)
                begun = jnp.where(even, 0, 2 if via else 1)
                go = (late == begun + hop) & (hop < 3) & jnp.logical_not(even & home)

                @pl.when(go)
                def _(j=j):
                    def at(s):
                        move(slot_of(j), j, s, cross).wait_recv()
                        move(slot_of(j), j, s, round_target(j)).start()

                    each(0, PIECES, at)

    def last(j):
        @pl.when(hop_of(j) == 3)
        def _():
            def at(s):
                move(slot_of(j), j, s, cross).wait_recv()

            each(0, PIECES, at)

    def product(pair):
        for j in range(8):
            if PAIR[j] == pair:
                last(j)
        first_slot = slot_of(PAIR.index(pair)) // 2 * 2
        rows = pl.ds(pl.multiple_of(first_slot * SHARD, 2 * SHARD), 2 * SHARD)

        def multiply(i):
            across = pl.ds(pl.multiple_of(i * 1024, 1024), 1024)
            block = lax.dot_general(
                panel[across, :], columns[rows, :], (((1,), (1,)), ((), ())), preferred_element_type=F32
            )
            gram_ref[across, rows] = block * F32(WIDTH * COLS)

        each(0, 2, multiply)

    def code(t, _):
        part = held[:, pl.ds(pl.multiple_of(t * WIDTH, WIDTH), WIDTH)]
        coded[t] = (part * scale).astype(BF16)
        return 0

    done = 0
    for step in range(STEPS):
        if step == 1:
            from_sibling(z, xl, False)
        for at_step, z_, xl_, half, sends, slot in arrivals:
            if at_step == step:
                gather(z_, xl_, half, sends, slot, xl_ is not xl)
        for at_step, z_, xl_, half, sends, slot in arrivals:
            if at_step == step:
                from_sibling(z_, xl_, xl_ is not xl)
        carry(step)
        if step == 2:
            lax.fori_loop(2, COLS, code, 0)
        if step == 8:
            def rest(n):
                block, s = n // PIECES, n % PIECES

                @pl.when((block % 2 == other) & jnp.logical_not(mine(block // 4)))
                def _():
                    arrived(block, s)

            each(0, PIECES * COLS, rest)

            @pl.when(home & even)
            def _():
                each(0, 8 * PIECES, lambda n: keep(core * 8 + n // PIECES, n % PIECES).wait())
        for i in range(done, done + ISSUE[step]):
            tile_start(i)
        done += ISSUE[step]

    for pair in (0, 1, 2, 3):
        product(pair)

    @pl.when(col >= 2)
    def _():
        tile_keep().start()
        each(1, COLS, lambda i: tile_recv(i).wait_recv())
        tile_keep().wait()

    @pl.when(col < 2)
    def _():
        def take(b):
            rows = pl.ds(pl.multiple_of(b * SHARD, SHARD), SHARD)
            tiles_ref[rows, :] = panel[rows, pl.ds(pl.multiple_of(core * WIDTH, WIDTH), WIDTH)]

        each(0, COLS, take)

    for i in range(len(TURNS)):

        @pl.when(partner(i) >= 2)
        def _(i=i):
            tile_send(i).wait_send()

    each(1, COLS, lambda i: send1(i).wait_send())
    each(1, ROWS, lambda i: send2(i).wait_send())

    def gone(s):
        for n in range(15):
            pass_on(own_block, s, n, sibling).wait_send()

    each(0, PIECES, gone)

    @pl.when(home)
    def _():
        each(0, 8 * PIECES, lambda n: lead(core * 8 + n // PIECES, n % PIECES, n // PIECES).wait_send())

    for j in range(8):
        if j % 4 < 2:

            @pl.when(bridge(j))
            def _(j=j):
                each(0, PIECES, lambda s: relay(j, s).wait_send())

        @pl.when((hop_of(j) < 3) & jnp.logical_not(even & home))
        def _(j=j):
            each(0, PIECES, lambda s: move(slot_of(j), j, s, cross).wait_send())


def shards(momentum):
    dma = pltpu.SemaphoreType.DMA
    return pl.pallas_call(
        kernel,
        out_shape=(
            pltpu.VMEM((COLS * SHARD, WIDTH), F32),
            pltpu.VMEM((COLS * SHARD, WIDTH), BF16),
        ),
        in_specs=[pl.BlockSpec(memory_space=pltpu.HBM)],
        out_specs=(
            pl.BlockSpec(memory_space=pltpu.VMEM),
            pl.BlockSpec(memory_space=pltpu.VMEM),
        ),
        scratch_shapes=[
            pltpu.VMEM((SHARD, COLS * WIDTH), F32),
            pltpu.VMEM((COLS, SHARD, WIDTH), BF16),
            pltpu.VMEM((COLS * SHARD, WINDOW), BF16),
            pltpu.VMEM((10 * SHARD, WINDOW), BF16),
            pltpu.VMEM((COLS, 8, 128), F32),
            pltpu.VMEM((ROWS, 8, 128), F32),
            dma((8,)),
            dma((COLS,)),
            dma((COLS,)),
            dma((ROWS,)),
            dma((ROWS,)),
            dma((COLS,)),
            dma((COLS,)),
            dma((15, PIECES)),
            dma((COLS, PIECES)),
            dma((8, PIECES)),
            dma((10, PIECES)),
            dma((10, PIECES)),
            dma((8, PIECES)),
        ],
        compiler_params=pltpu.CompilerParams(
            collective_id=0, has_side_effects=True, vmem_limit_bytes=36 * MIB
        ),
        cost_estimate=pl.CostEstimate(
            flops=2 * COLS * SHARD * WIDTH * WINDOW, bytes_accessed=20 * MIB, transcendentals=0
        ),
        name="newton_gram",
    )(momentum)


def solution(mesh):
    return jax.shard_map(
        shards,
        mesh=mesh,
        in_specs=(P(("row", "col"), None),),
        out_specs=(P("row", "col"), P("row", "col")),
        check_vma=False,
    )
```
